512 devices in a mesh: dp: 64 (over z, y), seq: 8 (over x, core).
Axes of the slice: x: 4, y: 4, z: 16, core: 2. Of those that a mesh axis runs over, the one named last changes fastest.
Arguments:
- queries: bfloat16 [65536, 1024], P(('dp', 'seq')), may hold values from -2.5 to 2.5
- key_vectors: bfloat16 [65536, 1024], P(('dp', 'seq')), may hold values from -2.5 to 2.5
- value_vectors: bfloat16 [65536, 1024], P(('dp', 'seq')), may hold values from -6 to 6
- gate_vectors: bfloat16 [65536, 1024], P(('dp', 'seq')), may hold values from -6 to 6
- out_grad: float32 [65536, 1024], P(('dp', 'seq')), may hold values from -24 to 24
- out_weight: float32 [1024, 1024], P('dp'), may hold values from -0.1875 to 0.1875
- time_bias: bfloat16 [128, 8], replicated, may hold values from -3 to 3
- lengths: int32 [64, 4], P('dp'), may hold values from 1 to 512, 1024 in all within a row
- stamps: int32 [65536], P(('dp', 'seq')), may hold values from 0 to 255, as said below
Outputs:
- query_grad: bfloat16 [65536, 1024], P(('dp', 'seq'))
- key_grad: bfloat16 [65536, 1024], P(('dp', 'seq'))
- value_grad: bfloat16 [65536, 1024], P(('dp', 'seq'))
- gate_grad: bfloat16 [65536, 1024], P(('dp', 'seq'))
- weight_grad: float32 [1024, 1024], P('dp')
The draws below stay inside these ranges and needn't reach their ends.
Inputs may be any that keep to these rules, and one draw needn't show every extreme that they name: Within each pack the stamps never fall from one event to the next; every pack has a first stamp of 0 and a last of 255. Each pack's 4 lengths sum to 1024, and the longest is exactly 512.
All inputs are finite; a program needn't handle non-finite values.
Results may differ from the reference program's by a relative error of at most 0.02.
Values may be sent and summed in bfloat16 or wider, within the bound.
A program may use at most 128 MiB of HBM per device.

```python
import math
import jax
import jax.numpy as jnp
import numpy as np
from jax import lax

D = 1024
HEADS = 8
BUCKETS = 128
SEQS = 4
TOK_DEV = 128
INNER = 1024
SLOTS = 1024
GROUPS = 64
TOKENS = 65536


def draw_stamps(key, part):
    key = jax.random.fold_in(key, 7)
    stamp_span = 2 * BUCKETS
    drawn = jax.random.randint(key, (GROUPS, SLOTS), 0, stamp_span, dtype=jnp.int32)
    ordered = jnp.sort(drawn, axis=1)
    ordered = ordered.at[:, 0].set(0).at[:, SLOTS - 1].set(stamp_span - 1)
    return ordered.reshape(TOKENS)


def spiked(values, rng, source, target, blocks, factor):
    owner, partner = [(jnp.arange(values.shape[axis_at]) // (values.shape[axis_at] // blocks)).reshape([-1 if axis == axis_at else 1 for axis in range(values.ndim)]) for axis_at in (source, target)]
    chosen = jax.random.permutation(rng, blocks)[partner]
    strong = (owner == chosen) | (owner == (partner + blocks // 2) % blocks)
    return jnp.where(strong, factor * values, values)


def shard_levels(stream_key, extent, split, smallest, high):
    loudness = 1.0
    for axis_at, parts in split:
        heights = jax.random.uniform(jax.random.fold_in(jax.random.fold_in(stream_key, 6), axis_at), (parts,), jnp.float32, smallest / len(split), high / len(split))
        loudness = loudness * jnp.repeat(jnp.exp(heights), extent[axis_at] // parts).reshape((-1,) + (1,) * (len(extent) - 1 - axis_at))
    return loudness


def length_profile(number_of, total, limit, lean):
    weights = [(1 << 20) // math.isqrt(rank ** lean) + 1 for rank in range(2, number_of + 1)]
    rest, given = total - limit - (number_of - 1), [1] * (number_of - 1)
    while rest > 0:
        free = [i for i in range(number_of - 1) if given[i] < limit]
        pool, budget = sum([weights[i] for i in free]), rest
        for i in free:
            extra = min(limit - given[i], max(1, budget * weights[i] // pool), rest)
            given[i] = given[i] + extra
            rest = rest - extra
    return np.array([limit] + given)


def ragged(rng, count, total, bound, lean):
    if count == 2:
        one = jax.random.randint(rng, (), max(1, total - bound), min(bound, total - 1) + 1)
        return jnp.stack([one, total - one])
    sizes = jnp.asarray(length_profile(count, total, bound, lean), jnp.int32)
    pairs = (count - 1) // 2
    donor, receiver = sizes[1:1 + 2 * pairs:2], sizes[2:2 + 2 * pairs:2]
    slack = jnp.minimum(donor - 1, bound - receiver)
    shifted = jax.random.randint(jax.random.fold_in(rng, 1), (pairs,), 0, 1 << 20) % (slack + 1)
    sizes = sizes.at[1:1 + 2 * pairs:2].set(donor - shifted).at[2:2 + 2 * pairs:2].set(receiver + shifted)
    return sizes[jax.random.permutation(jax.random.fold_in(rng, 2), count)]


def bell_draw(own_key, extent, deviation, reach, shards=(), kind=jnp.bfloat16):
    values = jax.random.normal(own_key, extent, jnp.float32) * deviation
    if len(shards) > 0:
        values = shard_levels(own_key, extent, shards, -0.22, 0.18) * values
    return jnp.clip(values, min=-reach, max=reach).astype(kind)


def bell_draw_with(own_key, dims, deviation, limit, pieces, heavy, held_as=jnp.bfloat16):
    entries = deviation * jax.random.normal(own_key, dims, jnp.float32)
    if pieces:
        entries = entries * shard_levels(own_key, dims, pieces, -0.22, 0.18)
    return jnp.clip(spiked(entries, jax.random.fold_in(own_key, 3), *heavy), -limit, limit).astype(held_as)


def setup_inputs(seed: int = 0) -> dict:
    key_of = jax.random.split(jax.random.key(seed), 10)
    return {
        "queries": bell_draw(key_of[0], (TOKENS, INNER), 0.35, 2.5, ((0, 512),)),
        "key_vectors": bell_draw(key_of[1], (TOKENS, INNER), 0.35, 2.5, ((0, 512),)),
        "value_vectors": bell_draw(key_of[2], (TOKENS, INNER), 1.0, 6.0, ((0, 512),)),
        "gate_vectors": bell_draw(key_of[3], (TOKENS, INNER), 1.0, 6.0, ((0, 512),)),
        "out_grad": bell_draw_with(key_of[4], (TOKENS, D), 1.0, 24.0, ((0, 512),), (0, 1, 512, 6.0), jnp.float32),
        "out_weight": bell_draw(key_of[5], (D, INNER), INNER ** -0.5, 0.1875, ((0, 64),), jnp.float32),
        "time_bias": bell_draw(key_of[6], (BUCKETS, HEADS), 0.7, 3.0),
        "lengths": jax.vmap(lambda own: ragged(own, SEQS, SLOTS, SLOTS // 2, 2))(jax.random.split(key_of[7], GROUPS)).reshape((GROUPS, SEQS)).astype(jnp.int32),
        "stamps": draw_stamps(jax.random.fold_in(key_of[9], 71), 0),
    }


norm_eps = 1e-06
exact = lax.Precision.HIGHEST

def silu_slope(scores):
    sigma = jax.nn.sigmoid(scores)
    return sigma * (1.0 + scores * (1.0 - sigma))

def one_pack(weight_sum, pack, out_weight, time_bias):
    queries, key_vectors, value_vectors, gate_vectors, out_grad, stamps, seq_lengths = pack
    slot_count = queries.shape[0]
    heads = time_bias.shape[1]
    query_heads = queries.astype(jnp.float32).reshape(slot_count, heads, -1)
    key_heads = key_vectors.astype(jnp.float32).reshape(slot_count, heads, -1)
    value_heads = value_vectors.astype(jnp.float32).reshape(slot_count, heads, -1)
    places = jnp.arange(slot_count, dtype=jnp.int32)
    ends = jnp.cumsum(seq_lengths, dtype=jnp.int32)
    segment = lax.optimization_barrier(jnp.sum((places[:, None] >= ends[None, :]).astype(jnp.int32), axis=1, dtype=jnp.int32))
    allowed = (segment[:, None] == segment[None, :]) & (places[None, :] <= places[:, None])
    bucket = jnp.clip(stamps[:, None] - stamps[None, :], 0, time_bias.shape[0] - 1)
    bias = jnp.transpose(time_bias.astype(jnp.float32)[bucket], (2, 0, 1))
    scores = jnp.einsum('qhd,khd->hqk', query_heads, key_heads, precision=exact) + bias
    probs = jnp.where(allowed[None], jax.nn.silu(scores), 0.0).astype(jnp.bfloat16)
    attended = jnp.einsum('hqk,khd->qhd', probs.astype(jnp.float32), value_heads, precision=exact).reshape(slot_count, -1)
    centred = attended - lax.optimization_barrier(jnp.mean(attended, axis=1, keepdims=True))
    inverse_scale = lax.rsqrt(lax.optimization_barrier(jnp.mean(centred * centred, axis=1, keepdims=True)) + norm_eps)
    normed = centred * inverse_scale
    gate_float = gate_vectors.astype(jnp.float32)
    gated = normed * gate_float
    gated_grad = jnp.dot(out_grad, out_weight, precision=exact, preferred_element_type=jnp.float32)
    weight_sum = weight_sum + jnp.dot(out_grad.T, gated, precision=exact, preferred_element_type=jnp.float32)
    gate_grad = (gated_grad * normed).astype(jnp.bfloat16)
    normed_grad = gated_grad * gate_float
    attended_grad = (inverse_scale * (normed_grad - lax.optimization_barrier(jnp.mean(normed_grad, axis=1, keepdims=True)) - normed * lax.optimization_barrier(jnp.mean(normed_grad * normed, axis=1, keepdims=True)))).astype(jnp.bfloat16)
    upstream = attended_grad.astype(jnp.float32).reshape(slot_count, heads, -1)
    probs_grad = jnp.einsum('qhd,khd->hqk', upstream, value_heads, precision=exact)
    scores_grad = jnp.where(allowed[None], probs_grad * silu_slope(scores), 0.0).astype(jnp.bfloat16)
    score_float = scores_grad.astype(jnp.float32)
    prob_float = probs.astype(jnp.float32)
    query_grad = jnp.einsum('hqk,khd->qhd', score_float, key_heads, precision=exact).reshape(slot_count, -1).astype(jnp.bfloat16)
    key_grad = jnp.einsum('hqk,qhd->khd', score_float, query_heads, precision=exact).reshape(slot_count, -1).astype(jnp.bfloat16)
    value_grad = jnp.einsum('hqk,qhd->khd', prob_float, upstream, precision=exact).reshape(slot_count, -1).astype(jnp.bfloat16)
    return (weight_sum, (query_grad, key_grad, value_grad, gate_grad))

def reference(queries, key_vectors, value_vectors, gate_vectors, out_grad, out_weight, time_bias, lengths, stamps):

    def by_pack(array):
        return array.reshape((GROUPS, SLOTS) + array.shape[1:])
    packs = (by_pack(queries), by_pack(key_vectors), by_pack(value_vectors), by_pack(gate_vectors), by_pack(out_grad), by_pack(stamps), lengths)

    def scan_step(weight_sum, pack):
        return one_pack(weight_sum, pack, out_weight, time_bias)
    weight_sum, grads = lax.scan(scan_step, jnp.zeros((D, INNER), jnp.float32), packs)
    query_grad = grads[0].reshape(TOKENS, INNER)
    key_grad = grads[1].reshape(TOKENS, INNER)
    value_grad = grads[2].reshape(TOKENS, INNER)
    gate_grad = grads[3].reshape(TOKENS, INNER)
    return (query_grad, key_grad, value_grad, gate_grad, weight_sum / TOK_DEV)
```

```python
import functools

import jax
import jax.numpy as jnp
from jax import lax
from jax.experimental import pallas as pl
from jax.experimental.pallas import tpu as pltpu
from jax.sharding import PartitionSpec as P

norm_eps = 1e-06
MESH = pl.DeviceIdType.MESH
F32 = jnp.float32
BF16 = jnp.bfloat16
T = 128
N = 8
NY = 4
NZ = 16
BAND = 4
NT = (((1,), (1,)), ((), ()))


def rows(i):
    return pl.ds(i * T, T)


def dyn(i):
    return pl.ds(pl.multiple_of(i * T, T), T)


def kernel(
    q_in, k_in, v_in, g_in, og_in, w_in, tb_in, len_in, st_in,
    dq_out, dk_out, dv_out, dg_out, wg_out,
    q, k, v, g, og, w, stamps, stats,
    kt, vt, gt, ngt, ggt, at, dat, gated, probs, slope, ds,
    dq, dk, dv, dg, wg, ry, zs, rz, fin,
    in_send, in_recv, w_send, w_recv, out_send, out_recv, own_sem,
):
    dp, me = lax.axis_index("dp"), lax.axis_index("seq")
    z, y = lax.div(dp, NY), lax.rem(dp, NY)

    def seq_peer(s):
        return (dp, s)

    def z_peer(zz):
        return (zz * NY + y, me)

    def y_peer(yy):
        return (z * NY + yy, me)

    def send(src, dst, ssem, rsem, device):
        pltpu.make_async_remote_copy(
            src_ref=src, dst_ref=dst, send_sem=ssem, recv_sem=rsem, device_id=device, device_id_type=MESH
        ).start()

    def wait(ref, sem):
        pltpu.make_async_copy(ref, ref, sem).wait()

    barrier = pltpu.get_barrier_semaphore()
    for d in range(1, N):
        pl.semaphore_signal(barrier, inc=1, device_id=seq_peer(lax.rem(me + d, N)), device_id_type=MESH)
    for d in range(1, NY):
        pl.semaphore_signal(barrier, inc=1, device_id=y_peer(lax.rem(y + d, NY)), device_id_type=MESH)
    for d in range(1, NZ):
        pl.semaphore_signal(barrier, inc=1, device_id=z_peer(lax.rem(z + d, NZ)), device_id_type=MESH)

    og[dyn(me), :] = og_in[...].astype(BF16)
    w[z, y] = w_in[:, dyn(me)].astype(BF16)
    stamps[me] = jnp.broadcast_to(st_in[...], (8, T))
    heads_of = tb_in[...].astype(F32)
    mine = jnp.where(lax.broadcasted_iota(jnp.int32, heads_of.shape, 1) == me, heads_of, 0.0)
    column = jnp.sum(mine, axis=1, keepdims=True)
    table = jnp.transpose(jnp.broadcast_to(column, (T, T)))

    pl.semaphore_wait(barrier, N - 1 + NY - 1 + NZ - 1)

    for d in range(1, N):
        peer = lax.rem(me + d, N)
        send(stamps.at[me], stamps.at[me], in_send.at[0], in_recv.at[0], seq_peer(peer))
    for n, (src, dst) in enumerate(((q_in, q), (k_in, k), (v_in, v))):
        pltpu.make_async_copy(src.at[:, dyn(me)], dst.at[dyn(me), :], in_recv.at[1 + n]).start()
        for d in range(1, N):
            peer = lax.rem(me + d, N)
            send(src.at[:, dyn(peer)], dst.at[dyn(me), :], in_send.at[1 + n], in_recv.at[1 + n], seq_peer(peer))
    for d in range(1, NZ):
        send(w.at[z, y], w.at[z, y], w_send.at[0], w_recv.at[0], z_peer(lax.rem(z + d, NZ)))
    for d in range(1, N):
        peer = lax.rem(me + d, N)
        send(og.at[dyn(me), :], og.at[dyn(me), :], in_send.at[5], in_recv.at[5], seq_peer(peer))
    pltpu.make_async_copy(g_in.at[:, dyn(me)], g.at[dyn(me), :], in_recv.at[4]).start()
    for d in range(1, N):
        peer = lax.rem(me + d, N)
        send(g_in.at[:, dyn(peer)], g.at[dyn(me), :], in_send.at[4], in_recv.at[4], seq_peer(peer))

    place = lax.broadcasted_iota(jnp.int32, (1, N * T), 1)
    end = jnp.int32(0)
    start = jnp.zeros((1, N * T), jnp.int32)
    for n in range(len_in.shape[1]):
        end = end + len_in[0, n]
        start = jnp.where(place >= end, end, start)
    below = lax.broadcasted_iota(jnp.int32, (T, T), 0)
    across = lax.broadcasted_iota(jnp.int32, (T, T), 1)

    wait(stamps.at[pl.ds(0, N - 1)], in_recv.at[0])
    wait(q, in_recv.at[1])
    wait(k, in_recv.at[2])
    for i in range(N):
        query_stamps = stamps[i, 0:1, :]
        for j in range(max(0, i - BAND), i + 1):
            key_stamps = jnp.transpose(jnp.broadcast_to(stamps[j, 0:1, :], (T, T)))
            bucket = jnp.clip(query_stamps - key_stamps, 0, T - 1)
            bias = jnp.take_along_axis(table, bucket, axis=1)
            score = lax.dot_general(k[rows(j), :], q[rows(i), :], NT, preferred_element_type=F32) + bias
            allowed = below >= start[:, i * T : (i + 1) * T] - j * T
            if i == j:
                allowed = allowed & (below <= across)
            sigma = jnp.where(allowed, 0.5 * jnp.tanh(0.5 * score) + 0.5, 0.0)
            prob = score * sigma
            probs[rows(j), rows(i)] = prob.astype(BF16)
            slope[rows(j), rows(i)] = sigma + prob * (1.0 - sigma)

    wait(w.at[pl.ds(0, NZ - 1), 0], w_recv.at[0])
    for d in range(1, NY):
        send(w.at[:, y], w.at[:, y], w_send.at[1], w_recv.at[1], y_peer(lax.rem(y + d, NY)))

    wait(v, in_recv.at[3])
    for i in range(N):
        vt[:, rows(i)] = jnp.transpose(v[rows(i), :])
        kt[:, rows(i)] = jnp.transpose(k[rows(i), :])
    for i in range(N):
        lo = max(0, i - BAND) * T
        hi = (i + 1) * T
        at[:, rows(i)] = jnp.dot(vt[:, lo:hi], probs[lo:hi, rows(i)], preferred_element_type=F32)

    wait(w.at[:, pl.ds(0, NY - 1)], w_recv.at[1])
    wait(og.at[pl.ds(0, (N - 1) * T), :], in_recv.at[5])
    wait(g, in_recv.at[4])
    weight = w[...].reshape(N * T, T)
    for i in range(N):
        gated_grad = jnp.transpose(jnp.dot(og[rows(i), :], weight, preferred_element_type=F32))
        gate = jnp.transpose(g[rows(i), :].astype(F32))
        normed_grad = gated_grad * gate
        attended = at[:, rows(i)]
        mean = jnp.sum(attended, axis=0, keepdims=True) * (1.0 / T)
        centred = attended - mean
        spread = jnp.sum(centred * centred, axis=0, keepdims=True)
        grad_sum = jnp.sum(normed_grad, axis=0, keepdims=True)
        cross = jnp.sum(normed_grad * centred, axis=0, keepdims=True)
        gt[:, rows(i)] = gate
        ggt[:, rows(i)] = gated_grad
        ngt[:, rows(i)] = normed_grad
        for n, value in enumerate((mean, spread, grad_sum, cross)):
            stats[me, 2 * n + i // 4 : 2 * n + i // 4 + 1, (i % 4) * T : (i % 4 + 1) * T] = value
    for d in range(1, N):
        send(stats.at[me], stats.at[me], in_send.at[6], in_recv.at[6], seq_peer(lax.rem(me + d, N)))
    wait(stats.at[pl.ds(0, N - 1)], in_recv.at[6])

    width = N * T
    for i in range(N):
        def stat(n):
            return stats[:, 2 * n + i // 4, (i % 4) * T : (i % 4 + 1) * T]

        means, grad_sums = stat(0), stat(2)
        mean = jnp.sum(means, axis=0, keepdims=True) * (1.0 / N)
        apart = means - mean
        spread = jnp.sum(stat(1), axis=0, keepdims=True) + T * jnp.sum(apart * apart, axis=0, keepdims=True)
        inverse = lax.rsqrt(spread * (1.0 / width) + norm_eps)
        grad_mean = jnp.sum(grad_sums, axis=0, keepdims=True) * (1.0 / width)
        cross = jnp.sum(stat(3) + apart * grad_sums, axis=0, keepdims=True) * inverse * (1.0 / width)
        normed = (at[:, rows(i)] - mean) * inverse
        gated[:, rows(i)] = (normed * gt[:, rows(i)]).astype(BF16)
        dat[:, rows(i)] = (inverse * (ngt[:, rows(i)] - grad_mean - normed * cross)).astype(BF16)
        dg[rows(i), :] = jnp.transpose(ggt[:, rows(i)] * normed).astype(BF16)

    def deliver(n, src, dst):
        pltpu.make_async_copy(src.at[dyn(me), :], dst.at[:, dyn(me)], out_recv.at[n]).start()
        for d in range(1, N):
            peer = lax.rem(me + d, N)
            send(src.at[dyn(peer), :], dst.at[:, dyn(me)], out_send.at[n], out_recv.at[n], seq_peer(peer))

    deliver(0, dg, dg_out)

    terms = jnp.dot(gated[...], og[...], preferred_element_type=F32)
    per = T // (NY * 16)
    for i in range(N):
        block = jnp.transpose(terms[:, i * T : (i + 1) * T]).astype(BF16)
        wg[i * per : (i + 1) * per] = block.reshape(per, NY, 16, T)
    ry[y] = wg[:, y]
    for d in range(1, NY):
        yy = lax.rem(y + d, NY)
        send(wg.at[:, yy], ry.at[y], w_send.at[2], w_recv.at[2], y_peer(yy))

    for j in range(N):
        lo, hi = j * T, min(j + BAND + 1, N) * T
        dv[rows(j), :] = lax.dot_general(
            probs[rows(j), lo:hi], dat[:, lo:hi], NT, preferred_element_type=F32
        ).astype(BF16)
    deliver(1, dv, dv_out)
    for i in range(N):
        lo, hi = max(0, i - BAND) * T, (i + 1) * T
        for j in range(max(0, i - BAND), i + 1):
            prob_grad = jnp.dot(v[rows(j), :], dat[:, rows(i)], preferred_element_type=F32)
            ds[rows(j), rows(i)] = (prob_grad * slope[rows(j), rows(i)]).astype(BF16)

    wait(ry.at[pl.ds(0, NY - 1)], w_recv.at[2])
    total = ry[0].astype(F32)
    for n in range(1, NY):
        total = total + ry[n].astype(F32)
    zs[...] = total.astype(BF16)
    rz[z] = zs[z]
    for d in range(1, NZ):
        zz = lax.rem(z + d, NZ)
        send(zs.at[zz], rz.at[z], w_send.at[3], w_recv.at[3], z_peer(zz))

    for i in range(N):
        lo, hi = max(0, i - BAND) * T, (i + 1) * T
        dq[rows(i), :] = jnp.transpose(
            jnp.dot(kt[:, lo:hi], ds[lo:hi, rows(i)], preferred_element_type=F32)
        ).astype(BF16)
    deliver(2, dq, dq_out)
    for j in range(N):
        lo, hi = j * T, min(j + BAND + 1, N) * T
        dk[rows(j), :] = jnp.dot(ds[rows(j), lo:hi], q[lo:hi, :], preferred_element_type=F32).astype(BF16)
    deliver(3, dk, dk_out)

    wait(rz.at[pl.ds(0, NZ - 1)], w_recv.at[3])
    total = rz[0].astype(F32)
    for n in range(1, NZ):
        total = total + rz[n].astype(F32)
    fin[...] = total * (1.0 / T)
    pltpu.make_async_copy(fin, wg_out.at[:, dyn(me)], own_sem).start()
    for d in range(1, N):
        send(fin, wg_out.at[:, dyn(me)], out_send.at[4], out_recv.at[4], seq_peer(lax.rem(me + d, N)))

    wait(stamps.at[pl.ds(0, N - 1)], in_send.at[0])
    for n in range(1, 5):
        wait(q.at[pl.ds(0, (N - 1) * T), :], in_send.at[n])
    wait(og.at[pl.ds(0, (N - 1) * T), :], in_send.at[5])
    wait(stats.at[pl.ds(0, N - 1)], in_send.at[6])
    wait(w.at[pl.ds(0, NZ - 1), 0], w_send.at[0])
    wait(w.at[:, pl.ds(0, NY - 1)], w_send.at[1])
    wait(ry.at[pl.ds(0, NY - 1)], w_send.at[2])
    wait(rz.at[pl.ds(0, NZ - 1)], w_send.at[3])
    for n, dst in enumerate((dg_out, dv_out, dq_out, dk_out)):
        wait(dst, out_recv.at[n])
        wait(q.at[pl.ds(0, (N - 1) * T), :], out_send.at[n])
    wait(fin, own_sem)
    wait(wg_out.at[:, pl.ds(0, (N - 1) * T)], out_recv.at[4])
    wait(wg_out.at[:, pl.ds(0, (N - 1) * T)], out_send.at[4])


def shards(queries, keys, values, gates, out_grad, out_weight, time_bias, lengths, stamps):
    width = N * T
    event = jax.ShapeDtypeStruct((T, width), BF16)
    block = pltpu.VMEM((width, T), BF16)
    across16 = pltpu.VMEM((T, width), BF16)
    across32 = pltpu.VMEM((T, width), F32)
    hbm = pl.BlockSpec(memory_space=pl.ANY)
    vmem = pl.BlockSpec(memory_space=pltpu.VMEM)
    smem = pl.BlockSpec(memory_space=pltpu.SMEM)
    return pl.pallas_call(
        kernel,
        out_shape=(event, event, event, event, jax.ShapeDtypeStruct((16, width), F32)),
        in_specs=[hbm, hbm, hbm, hbm, vmem, vmem, vmem, smem, vmem],
        out_specs=(hbm,) * 5,
        scratch_shapes=[
            block, block, block, block,
            pltpu.VMEM((width, width), BF16),
            pltpu.VMEM((NZ, NY, 16, T), BF16),
            pltpu.VMEM((N, 8, T), jnp.int32),
            pltpu.VMEM((N, 8, 4 * T), F32),
            across16, across16,
            across32, across32, across32, across32,
            across16, across16,
            pltpu.VMEM((width, width), BF16),
            pltpu.VMEM((width, width), F32),
            pltpu.VMEM((width, width), BF16),
            block, block, block, block,
            pltpu.VMEM((NZ, NY, 16, T), BF16),
            pltpu.VMEM((NY, NZ, 16, T), BF16),
            pltpu.VMEM((NZ, 16, T), BF16),
            pltpu.VMEM((NZ, 16, T), BF16),
            pltpu.VMEM((16, T), F32),
            pltpu.SemaphoreType.DMA((7,)),
            pltpu.SemaphoreType.DMA((7,)),
            pltpu.SemaphoreType.DMA((4,)),
            pltpu.SemaphoreType.DMA((4,)),
            pltpu.SemaphoreType.DMA((5,)),
            pltpu.SemaphoreType.DMA((5,)),
            pltpu.SemaphoreType.DMA,
        ],
        compiler_params=pltpu.CompilerParams(
            collective_id=0, has_side_effects=True, vmem_limit_bytes=48 * 1024 * 1024
        ),
    )(queries, keys, values, gates, out_grad, out_weight, time_bias, lengths, stamps.reshape(1, T))


def solution(mesh):
    events = P(("dp", "seq"), None)
    return jax.shard_map(
        shards,
        mesh=mesh,
        in_specs=(
            events, events, events, events, events, P("dp", None), P(), P("dp", None), P(("dp", "seq")),
        ),
        out_specs=(events, events, events, events, P("dp", None)),
        check_vma=False,
    )
```

```python
import functools

import jax
import jax.numpy as jnp
from jax import lax
from jax.experimental import pallas as pl
from jax.experimental.pallas import tpu as pltpu
from jax.sharding import PartitionSpec as P

norm_eps = 1e-06
MESH = pl.DeviceIdType.MESH
F32 = jnp.float32
BF16 = jnp.bfloat16
T = 128
N = 8
NY = 4
NZ = 16
BAND = 4
NT = (((1,), (1,)), ((), ()))


def rows(i):
    return pl.ds(i * T, T)


def dyn(i):
    return pl.ds(pl.multiple_of(i * T, T), T)


def kernel(
    q_in, k_in, v_in, g_in, og_hbm, w_hbm, tb_hbm, len_hbm, st_hbm,
    dq_out, dk_out, dv_out, dg_out, wg_out,
    q, k, v, g, og, w, stamps, stats,
    kt, vt, gt, ngt, ggt, at, dat, gated, probs, slope, ds,
    dq, dk, dv, dg, wg, ry, zs, rz, fin,
    og_in, w_in, tb_in, len_in, st_in,
    in_send, in_recv, og_send, og_recv, w_send, w_recv, out_send, out_recv, own_sem, load_sem,
):
    dp, me = lax.axis_index("dp"), lax.axis_index("seq")
    z, y = lax.div(dp, NY), lax.rem(dp, NY)

    def seq_peer(s):
        return (dp, s)

    def z_peer(zz):
        return (zz * NY + y, me)

    def y_peer(yy):
        return (z * NY + yy, me)

    chip, core = lax.div(me, 2), lax.rem(me, 2)
    left, right = lax.rem(me + N - 2, N), lax.rem(me + 2, N)
    facing = lax.rem(me + 4, N)
    sibling = 2 * chip + 1 - core

    def half(owner, part):
        return og.at[pl.ds(pl.multiple_of(owner * T + part * (T // 2), T // 2), T // 2), :]

    def pass_on(n, owner, part, peer):
        ref = half(owner, part)
        send(ref, ref, og_send.at[n], og_recv.at[n], seq_peer(peer))
        expect('og%d' % n, half(0, 0), og_recv.at[n])
        expect('og%d sent' % n, half(0, 0), og_send.at[n])

    def send(src, dst, ssem, rsem, device):
        pltpu.make_async_remote_copy(
            src_ref=src, dst_ref=dst, send_sem=ssem, recv_sem=rsem, device_id=device, device_id_type=MESH
        ).start()

    expected = {}

    def expect(name, ref, sem):
        expected[name] = (ref, sem)

    def wait(name):
        ref, sem = expected.pop(name)
        pltpu.make_async_copy(ref, ref, sem).wait()

    loads = [
        pltpu.make_async_copy(src, dst, load_sem.at[n])
        for n, (src, dst) in enumerate(((og_hbm, og_in), (w_hbm, w_in), (tb_hbm, tb_in), (len_hbm, len_in), (st_hbm, st_in)))
    ]
    for load in loads:
        load.start()

    barrier = pltpu.get_barrier_semaphore()
    for d in range(1, N):
        pl.semaphore_signal(barrier, inc=1, device_id=seq_peer(lax.rem(me + d, N)), device_id_type=MESH)
    for d in range(1, NY):
        pl.semaphore_signal(barrier, inc=1, device_id=y_peer(lax.rem(y + d, NY)), device_id_type=MESH)
    for d in range(1, NZ):
        pl.semaphore_signal(barrier, inc=1, device_id=z_peer(lax.rem(z + d, NZ)), device_id_type=MESH)

    for load in loads:
        load.wait()
    og[dyn(me), :] = og_in[...].astype(BF16)
    w[z, y] = w_in[:, dyn(me)].astype(BF16)
    stamps[me] = jnp.broadcast_to(st_in[...], (8, T))
    heads_of = tb_in[...].astype(F32)
    mine = jnp.where(lax.broadcasted_iota(jnp.int32, heads_of.shape, 0) == me, heads_of, 0.0)
    table = jnp.broadcast_to(jnp.sum(mine, axis=0, keepdims=True), (T, T))

    pl.semaphore_wait(barrier, N - 1 + NY - 1 + NZ - 1)

    for d in range(1, N):
        peer = lax.rem(me + d, N)
        send(stamps.at[me], stamps.at[me], in_send.at[0], in_recv.at[0], seq_peer(peer))
    expect('stamps', stamps.at[pl.ds(0, N - 1)], in_recv.at[0])
    expect('stamps sent', stamps.at[pl.ds(0, N - 1)], in_send.at[0])
    for n, (src, dst) in enumerate(((q_in, q), (k_in, k), (v_in, v))):
        pltpu.make_async_copy(src.at[:, dyn(me)], dst.at[dyn(me), :], in_recv.at[1 + n]).start()
        for d in range(1, N):
            peer = lax.rem(me + d, N)
            send(src.at[:, dyn(peer)], dst.at[dyn(me), :], in_send.at[1 + n], in_recv.at[1 + n], seq_peer(peer))
        expect('qkv'[n], dst, in_recv.at[1 + n])
        expect('qkv'[n] + ' sent', q.at[pl.ds(0, (N - 1) * T), :], in_send.at[1 + n])
    for d in range(1, NZ):
        send(w.at[z, y], w.at[z, y], w_send.at[0], w_recv.at[0], z_peer(lax.rem(z + d, NZ)))
    expect('w z', w.at[pl.ds(0, NZ - 1), 0], w_recv.at[0])
    expect('w z sent', w.at[pl.ds(0, NZ - 1), 0], w_send.at[0])
    pass_on(0, me, 0, right)
    pass_on(1, me, 1, left)
    pass_on(2, me, 1, right)
    pass_on(3, me, 0, left)
    pass_on(6, me, 0, sibling)
    pass_on(7, me, 1, sibling)
    pltpu.make_async_copy(g_in.at[:, dyn(me)], g.at[dyn(me), :], in_recv.at[4]).start()
    for d in range(1, N):
        peer = lax.rem(me + d, N)
        send(g_in.at[:, dyn(peer)], g.at[dyn(me), :], in_send.at[4], in_recv.at[4], seq_peer(peer))

    expect('g', g, in_recv.at[4])
    expect('g sent', q.at[pl.ds(0, (N - 1) * T), :], in_send.at[4])
    place = lax.broadcasted_iota(jnp.int32, (1, N * T), 1)
    end = jnp.int32(0)
    start = jnp.zeros((1, N * T), jnp.int32)
    for n in range(len_in.shape[1]):
        end = end + len_in[0, n]
        start = jnp.where(place >= end, end, start)
    below = lax.broadcasted_iota(jnp.int32, (T, T), 0)
    across = lax.broadcasted_iota(jnp.int32, (T, T), 1)

    wait('stamps')
    wait('q')
    wait('k')
    for i in range(N):
        query_stamps = stamps[i, 0:1, :]
        for j in range(max(0, i - BAND), i + 1):
            key_stamps = jnp.transpose(jnp.broadcast_to(stamps[j, 0:1, :], (T, T)))
            bucket = jnp.clip(query_stamps - key_stamps, 0, T - 1)
            bias = jnp.take_along_axis(table, bucket, axis=1)
            score = lax.dot_general(k[rows(j), :], q[rows(i), :], NT, preferred_element_type=F32) + bias
            allowed = below >= start[:, i * T : (i + 1) * T] - j * T
            if i == j:
                allowed = allowed & (below <= across)
            sigma = jnp.where(allowed, 0.5 * jnp.tanh(0.5 * score) + 0.5, 0.0)
            prob = score * sigma
            probs[rows(j), rows(i)] = prob.astype(BF16)
            slope[rows(j), rows(i)] = sigma + prob * (1.0 - sigma)

    wait('og0')
    pass_on(4, left, 0, right)
    wait('og1')
    pass_on(5, right, 1, left)
    pass_on(8, left, 0, sibling)
    pass_on(9, right, 1, sibling)
    wait('og2')
    pass_on(10, left, 1, sibling)
    wait('og3')
    pass_on(11, right, 0, sibling)
    wait('w z')
    for d in range(1, NY):
        send(w.at[:, y], w.at[:, y], w_send.at[1], w_recv.at[1], y_peer(lax.rem(y + d, NY)))
    expect('w y', w.at[:, pl.ds(0, NY - 1)], w_recv.at[1])
    expect('w y sent', w.at[:, pl.ds(0, NY - 1)], w_send.at[1])

    wait('v')
    for i in range(N):
        vt[:, rows(i)] = jnp.transpose(v[rows(i), :])
        kt[:, rows(i)] = jnp.transpose(k[rows(i), :])
    for i in range(N):
        lo = max(0, i - BAND) * T
        hi = (i + 1) * T
        at[:, rows(i)] = jnp.dot(vt[:, lo:hi], probs[lo:hi, rows(i)], preferred_element_type=F32)

    wait('w y')
    wait('og4')
    pass_on(12, facing, 0, sibling)
    wait('og5')
    pass_on(13, facing, 1, sibling)
    for n in range(6, 14):
        wait('og%d' % n)
    wait('g')
    weight = w[...].reshape(N * T, T)
    for i in range(N):
        gated_grad = jnp.transpose(jnp.dot(og[rows(i), :], weight, preferred_element_type=F32))
        gate = jnp.transpose(g[rows(i), :].astype(F32))
        normed_grad = gated_grad * gate
        attended = at[:, rows(i)]
        mean = jnp.sum(attended, axis=0, keepdims=True) * (1.0 / T)
        centred = attended - mean
        spread = jnp.sum(centred * centred, axis=0, keepdims=True)
        grad_sum = jnp.sum(normed_grad, axis=0, keepdims=True)
        cross = jnp.sum(normed_grad * centred, axis=0, keepdims=True)
        gt[:, rows(i)] = gate
        ggt[:, rows(i)] = gated_grad
        ngt[:, rows(i)] = normed_grad
        for n, value in enumerate((mean, spread, grad_sum, cross)):
            stats[me, 2 * n + i // 4 : 2 * n + i // 4 + 1, (i % 4) * T : (i % 4 + 1) * T] = value
    for d in range(1, N):
        send(stats.at[me], stats.at[me], in_send.at[6], in_recv.at[6], seq_peer(lax.rem(me + d, N)))
    expect('stats', stats.at[pl.ds(0, N - 1)], in_recv.at[6])
    expect('stats sent', stats.at[pl.ds(0, N - 1)], in_send.at[6])
    wait('stats')

    width = N * T
    for i in range(N):
        def stat(n):
            return stats[:, 2 * n + i // 4, (i % 4) * T : (i % 4 + 1) * T]

        means, grad_sums = stat(0), stat(2)
        mean = jnp.sum(means, axis=0, keepdims=True) * (1.0 / N)
        apart = means - mean
        spread = jnp.sum(stat(1), axis=0, keepdims=True) + T * jnp.sum(apart * apart, axis=0, keepdims=True)
        inverse = lax.rsqrt(spread * (1.0 / width) + norm_eps)
        grad_mean = jnp.sum(grad_sums, axis=0, keepdims=True) * (1.0 / width)
        cross = jnp.sum(stat(3) + apart * grad_sums, axis=0, keepdims=True) * inverse * (1.0 / width)
        normed = (at[:, rows(i)] - mean) * inverse
        gated[:, rows(i)] = (normed * gt[:, rows(i)]).astype(BF16)
        dat[:, rows(i)] = (inverse * (ngt[:, rows(i)] - grad_mean - normed * cross)).astype(BF16)
        dg[rows(i), :] = jnp.transpose(ggt[:, rows(i)] * normed).astype(BF16)

    def deliver(n, src, dst):
        pltpu.make_async_copy(src.at[dyn(me), :], dst.at[:, dyn(me)], out_recv.at[n]).start()
        for d in range(1, N):
            peer = lax.rem(me + d, N)
            send(src.at[dyn(peer), :], dst.at[:, dyn(me)], out_send.at[n], out_recv.at[n], seq_peer(peer))
        expect('out%d' % n, dst, out_recv.at[n])
        expect('out%d sent' % n, q.at[pl.ds(0, (N - 1) * T), :], out_send.at[n])

    deliver(0, dg, dg_out)

    terms = jnp.dot(gated[...], og[...], preferred_element_type=F32)
    per = T // (NY * 16)
    for i in range(N):
        block = jnp.transpose(terms[:, i * T : (i + 1) * T]).astype(BF16)
        wg[i * per : (i + 1) * per] = block.reshape(per, NY, 16, T)
    ry[y] = wg[:, y]
    for d in range(1, NY):
        yy = lax.rem(y + d, NY)
        send(wg.at[:, yy], ry.at[y], w_send.at[2], w_recv.at[2], y_peer(yy))
    expect('ry', ry.at[pl.ds(0, NY - 1)], w_recv.at[2])
    expect('ry sent', ry.at[pl.ds(0, NY - 1)], w_send.at[2])

    for j in range(N):
        lo, hi = j * T, min(j + BAND + 1, N) * T
        dv[rows(j), :] = lax.dot_general(
            probs[rows(j), lo:hi], dat[:, lo:hi], NT, preferred_element_type=F32
        ).astype(BF16)
    deliver(1, dv, dv_out)
    for i in range(N):
        lo, hi = max(0, i - BAND) * T, (i + 1) * T
        for j in range(max(0, i - BAND), i + 1):
            prob_grad = jnp.dot(v[rows(j), :], dat[:, rows(i)], preferred_element_type=F32)
            ds[rows(j), rows(i)] = (prob_grad * slope[rows(j), rows(i)]).astype(BF16)

    wait('ry')
    total = ry[0].astype(F32)
    for n in range(1, NY):
        total = total + ry[n].astype(F32)
    zs[...] = total.astype(BF16)
    rz[z] = zs[z]
    for d in range(1, NZ):
        zz = lax.rem(z + d, NZ)
        send(zs.at[zz], rz.at[z], w_send.at[3], w_recv.at[3], z_peer(zz))
    expect('rz', rz.at[pl.ds(0, NZ - 1)], w_recv.at[3])
    expect('rz sent', rz.at[pl.ds(0, NZ - 1)], w_send.at[3])

    for i in range(N):
        lo, hi = max(0, i - BAND) * T, (i + 1) * T
        dq[rows(i), :] = jnp.transpose(
            jnp.dot(kt[:, lo:hi], ds[lo:hi, rows(i)], preferred_element_type=F32)
        ).astype(BF16)
    deliver(2, dq, dq_out)
    for j in range(N):
        lo, hi = j * T, min(j + BAND + 1, N) * T
        dk[rows(j), :] = jnp.dot(ds[rows(j), lo:hi], q[lo:hi, :], preferred_element_type=F32).astype(BF16)
    deliver(3, dk, dk_out)

    wait('rz')
    total = rz[0].astype(F32)
    for n in range(1, NZ):
        total = total + rz[n].astype(F32)
    fin[...] = total * (1.0 / T)
    pltpu.make_async_copy(fin, wg_out.at[:, dyn(me)], own_sem).start()
    for d in range(1, N):
        send(fin, wg_out.at[:, dyn(me)], out_send.at[4], out_recv.at[4], seq_peer(lax.rem(me + d, N)))

    rest = wg_out.at[:, pl.ds(0, (N - 1) * T)]
    expect('fin', fin, own_sem)
    expect('out4', rest, out_recv.at[4])
    expect('out4 sent', rest, out_send.at[4])

    for name in list(expected):
        wait(name)


def settle(*refs):
    sems = refs[10]
    copies = [pltpu.make_async_copy(refs[n], refs[5 + n], sems.at[n]) for n in range(5)]
    for copy in copies:
        copy.start()
    for copy in copies:
        copy.wait()


def shards(queries, keys, values, gates, out_grad, out_weight, time_bias, lengths, stamps):
    width = N * T
    event = pltpu.VMEM((T, width), BF16)
    block = pltpu.VMEM((width, T), BF16)
    across16 = pltpu.VMEM((T, width), BF16)
    across32 = pltpu.VMEM((T, width), F32)
    hbm = pl.BlockSpec(memory_space=pl.ANY)
    away = pl.BlockSpec(memory_space=pltpu.HBM)
    outs = pl.pallas_call(
        kernel,
        out_shape=(event, event, event, event, pltpu.VMEM((16, width), F32)),
        in_specs=[hbm] * 9,
        out_specs=(hbm,) * 5,
        scratch_shapes=[
            block, block, block, block,
            pltpu.VMEM((width, width), BF16),
            pltpu.VMEM((NZ, NY, 16, T), BF16),
            pltpu.VMEM((N, 8, T), jnp.int32),
            pltpu.VMEM((N, 8, 4 * T), F32),
            across16, across16,
            across32, across32, across32, across32,
            across16, across16,
            pltpu.VMEM((width, width), BF16),
            pltpu.VMEM((width, width), F32),
            pltpu.VMEM((width, width), BF16),
            block, block, block, block,
            pltpu.VMEM((NZ, NY, 16, T), BF16),
            pltpu.VMEM((NY, NZ, 16, T), BF16),
            pltpu.VMEM((NZ, 16, T), BF16),
            pltpu.VMEM((NZ, 16, T), BF16),
            pltpu.VMEM((16, T), F32),
            pltpu.VMEM((T, width), F32), pltpu.VMEM((16, width), F32), pltpu.VMEM((8, T), BF16),
            pltpu.SMEM((1, 4), jnp.int32), pltpu.VMEM((1, T), jnp.int32),
            pltpu.SemaphoreType.DMA((7,)),
            pltpu.SemaphoreType.DMA((7,)),
            pltpu.SemaphoreType.DMA((14,)),
            pltpu.SemaphoreType.DMA((14,)),
            pltpu.SemaphoreType.DMA((4,)),
            pltpu.SemaphoreType.DMA((4,)),
            pltpu.SemaphoreType.DMA((5,)),
            pltpu.SemaphoreType.DMA((5,)),
            pltpu.SemaphoreType.DMA,
            pltpu.SemaphoreType.DMA((5,)),
        ],
        compiler_params=pltpu.CompilerParams(
            collective_id=0, has_side_effects=True, vmem_limit_bytes=48 * 1024 * 1024
        ),
    )(
        *(
            pltpu.with_memory_space_constraint(a, pltpu.HBM)
            for a in (queries, keys, values, gates, out_grad, out_weight, time_bias.T, lengths, stamps.reshape(1, T))
        )
    )
    return pl.pallas_call(
        settle,
        out_shape=[jax.ShapeDtypeStruct(o.shape, o.dtype) for o in outs],
        in_specs=[hbm] * 5,
        out_specs=[away] * 5,
        scratch_shapes=[pltpu.SemaphoreType.DMA((5,))],
        compiler_params=pltpu.CompilerParams(vmem_limit_bytes=4 * 1024 * 1024),
    )(*(pltpu.with_memory_space_constraint(o, pltpu.VMEM) for o in outs))


def solution(mesh):
    events = P(("dp", "seq"), None)
    return jax.shard_map(
        shards,
        mesh=mesh,
        in_specs=(
            events, events, events, events, events, P("dp", None), P(), P("dp", None), P(("dp", "seq")),
        ),
        out_specs=(events, events, events, events, P("dp", None)),
        check_vma=False,
    )
```

```python
import functools

import jax
import jax.numpy as jnp
from jax import lax
from jax.experimental import pallas as pl
from jax.experimental.pallas import tpu as pltpu
from jax.sharding import PartitionSpec as P

norm_eps = 1e-06
MESH = pl.DeviceIdType.MESH
F32 = jnp.float32
BF16 = jnp.bfloat16
T = 128
N = 8
NY = 4
NZ = 16
HUB = 11
BAND = 4
NT = (((1,), (1,)), ((), ()))


def rows(i):
    return pl.ds(i * T, T)


def dyn(i):
    return pl.ds(pl.multiple_of(i * T, T), T)


def kernel(
    q_in, k_in, v_in, g_in, og_hbm, w_hbm, tb_hbm, len_hbm, st_hbm,
    dq_out, dk_out, dv_out, dg_out, wg_out,
    q, k, v, g, og, w, stamps, stats, grad_stats,
    kt, vt, ngt, gt, at, dat, gated, normed, probs, slope, ds,
    dq, dk, dv, dg, wg, ry, zs, rz, fin,
    og_in, w_in, tb_in, len_in, st_in,
    in_send, in_recv, og_send, og_recv, w_send, w_recv, out_send, out_recv, own_sem, load_sem, ready,
):
    dp, me = lax.axis_index("dp"), lax.axis_index("seq")
    z, y = lax.div(dp, NY), lax.rem(dp, NY)
    chip, core = lax.div(me, 2), lax.rem(me, 2)
    left, right = lax.rem(me + N - 2, N), lax.rem(me + 2, N)
    facing = lax.rem(me + 4, N)
    sibling = 2 * chip + 1 - core
    width = N * T

    def seq_peer(s):
        return (dp, s)

    def z_peer(zz):
        return (zz * NY + y, me)

    def y_peer(yy):
        return (z * NY + yy, me)

    def send(src, dst, ssem, rsem, device):
        pltpu.make_async_remote_copy(
            src_ref=src, dst_ref=dst, send_sem=ssem, recv_sem=rsem, device_id=device, device_id_type=MESH
        ).start()

    def greet(first, last, sem, peer):
        def one(n, carry):
            pl.semaphore_signal(sem, inc=1, device_id=peer(n), device_id_type=MESH)
            return carry

        lax.fori_loop(first, last, one, 0)

    expected = {}

    def expect(name, ref, sem):
        expected[name] = (ref, sem)

    def wait(name):
        ref, sem = expected.pop(name)
        pltpu.make_async_copy(ref, ref, sem).wait()

    others = q.at[pl.ds(0, (N - 1) * T), :]

    def collect(n, src, dst):
        pltpu.make_async_copy(src.at[:, dyn(me)], dst.at[dyn(me), :], in_recv.at[n]).start()
        for d in range(1, N):
            peer = lax.rem(me + d, N)
            send(src.at[:, dyn(peer)], dst.at[dyn(me), :], in_send.at[n], in_recv.at[n], seq_peer(peer))

    def share(name, n, ref):
        for d in range(1, N):
            send(ref.at[me], ref.at[me], in_send.at[n], in_recv.at[n], seq_peer(lax.rem(me + d, N)))
        expect(name, ref.at[pl.ds(0, N - 1)], in_recv.at[n])
        expect(name + ' sent', ref.at[pl.ds(0, N - 1)], in_send.at[n])

    def deliver(name, n, src, dst):
        pltpu.make_async_copy(src.at[dyn(me), :], dst.at[:, dyn(me)], out_recv.at[n]).start()
        for d in range(1, N):
            peer = lax.rem(me + d, N)
            send(src.at[dyn(peer), :], dst.at[:, dyn(me)], out_send.at[n], out_recv.at[n], seq_peer(peer))
        expect(name, dst, out_recv.at[n])
        expect(name + ' sent', others, out_send.at[n])

    columns = [pl.ds(n * 2 * T, 2 * T) for n in range(4)]
    parts = [pl.ds(n * 4, 4) for n in range(4)]

    def pass_on(kind, n, owner, first, count, peer):
        ref = og.at[pl.ds(pl.multiple_of(owner * T + first, T // 2), count), columns[n]]
        send(ref, ref, og_send.at[4 * kind + n], og_recv.at[4 * kind + n], seq_peer(peer))

    def expect_part(kind, n, count):
        size = og.at[pl.ds(0, count), pl.ds(0, 2 * T)]
        expect('og%d-%d' % (kind, n), size, og_recv.at[4 * kind + n])
        expect('og%d-%d sent' % (kind, n), size, og_send.at[4 * kind + n])

    loads = [
        pltpu.make_async_copy(src, dst, load_sem.at[n])
        for n, (src, dst) in enumerate(
            ((og_hbm, og_in), (w_hbm, w_in), (tb_hbm, tb_in), (len_hbm, len_in), (st_hbm, st_in))
        )
    ]
    for load in loads:
        load.start()

    barrier = pltpu.get_barrier_semaphore()
    for d in range(1, N):
        pl.semaphore_signal(barrier, inc=1, device_id=seq_peer(lax.rem(me + d, N)), device_id_type=MESH)
    greet(y + 1, NY, barrier, y_peer)

    @pl.when(z != HUB)
    def _():
        pl.semaphore_signal(barrier, inc=1, device_id=z_peer(HUB), device_id_type=MESH)

    for load in loads:
        load.wait()
    og[dyn(me), :] = og_in[...].astype(BF16)
    stamps[me] = st_in[...]
    w[z, y] = w_in[:, dyn(me)].astype(BF16)

    pl.semaphore_wait(barrier, N - 1 + y + jnp.where(z == HUB, NZ - 1, 0))
    share('stamps', 0, stamps)
    collect(1, q_in, q)
    greet(0, y, ready, y_peer)

    @pl.when(z == HUB)
    def _():
        for d in range(1, NZ):
            pl.semaphore_signal(ready, inc=1, device_id=z_peer(lax.rem(z + d, NZ)), device_id_type=MESH)

    heads_of = tb_in[...].astype(F32)
    mine = jnp.where(lax.broadcasted_iota(jnp.int32, heads_of.shape, 0) == me, heads_of, 0.0)
    table = jnp.broadcast_to(jnp.sum(mine, axis=0, keepdims=True), (T, T))
    place = lax.broadcasted_iota(jnp.int32, (1, N * T), 1)
    end = jnp.int32(0)
    start = jnp.zeros((1, N * T), jnp.int32)
    for n in range(len_in.shape[1]):
        end = end + len_in[0, n]
        start = jnp.where(place >= end, end, start)
    below = lax.broadcasted_iota(jnp.int32, (T, T), 0)
    across = lax.broadcasted_iota(jnp.int32, (T, T), 1)
    def spread_weight():
        answers = NY - 1 - y + jnp.where(z == HUB, 0, 1)

        @pl.when(answers > 0)
        def _():
            pl.semaphore_wait(ready, answers)

        for d in range(1, NZ):
            send(w.at[z, y], w.at[z, y], w_send.at[0], w_recv.at[0], z_peer(lax.rem(z + d, NZ)))

    def start_ring():
        pass_on(0, 0, me, 0, T, right)
        pass_on(1, 0, me, 0, T, left)
        pass_on(5, 0, me, 0, T, facing)
        pass_on(2, 0, me, 0, T, sibling)

    @pl.when(z < NZ // 4)
    def _():
        collect(2, k_in, k)
        collect(3, v_in, v)
        collect(4, g_in, g)
        start_ring()

    @pl.when((z >= NZ // 4) & (z < NZ // 2))
    def _():
        collect(2, k_in, k)
        collect(3, v_in, v)
        spread_weight()
        collect(4, g_in, g)
        start_ring()

    @pl.when(z >= NZ // 2)
    def _():
        collect(2, k_in, k)
        spread_weight()
        collect(3, v_in, v)
        collect(4, g_in, g)
        start_ring()

    for n, (name, dst) in enumerate((('q', q), ('k', k), ('v', v), ('g', g))):
        expect(name, dst, in_recv.at[1 + n])
        expect(name + ' sent', others, in_send.at[1 + n])
    for kind in (0, 1, 5, 2):
        expect_part(kind, 0, T)
    expect('w z', w.at[pl.ds(0, NZ - 1), 0], w_recv.at[0])
    expect('w z sent', w.at[pl.ds(0, NZ - 1), 0], w_send.at[0])

    wait('stamps')
    wait('q')
    wait('k')
    for i in range(N):
        query_stamps = stamps[i, 0:1, :]
        for j in range(max(0, i - BAND), i + 1):
            key_stamps = jnp.transpose(jnp.broadcast_to(stamps[j, 0:1, :], (T, T)))
            bucket = jnp.clip(query_stamps - key_stamps, 0, T - 1)
            bias = jnp.take_along_axis(table, bucket, axis=1)
            score = lax.dot_general(k[rows(j), :], q[rows(i), :], NT, preferred_element_type=F32) + bias
            allowed = below >= start[:, i * T : (i + 1) * T] - j * T
            if i == j:
                allowed = allowed & (below <= across)
            sigma = jnp.where(allowed, 0.5 * jnp.tanh(0.5 * score) + 0.5, 0.0)
            prob = score * sigma
            probs[rows(j), rows(i)] = prob.astype(BF16)
            slope[rows(j), rows(i)] = sigma + prob * (1.0 - sigma)

    wait('v')
    for i in range(N):
        vt[:, rows(i)] = jnp.transpose(v[rows(i), :])
        kt[:, rows(i)] = jnp.transpose(k[rows(i), :])

    def put(ref, n, i, value):
        row, col = 4 * n + i // 2, (i % 2) * T
        ref[me, row : row + 1, col : col + T] = value

    def get(ref, n, i):
        row, col = 4 * n + i // 2, (i % 2) * T
        return ref[:, row, col : col + T]

    for i in range(N):
        lo, hi = max(0, i - BAND) * T, (i + 1) * T
        attended = jnp.dot(vt[:, lo:hi], probs[lo:hi, rows(i)], preferred_element_type=F32)
        at[:, rows(i)] = attended
        mean = jnp.sum(attended, axis=0, keepdims=True) * (1.0 / T)
        centred = attended - mean
        put(stats, 0, i, mean)
        put(stats, 1, i, jnp.sum(centred * centred, axis=0, keepdims=True))
    share('stats', 5, stats)
    pl.when(z < NZ // 4)(spread_weight)
    for n in range(1, 4):
        pass_on(0, n, me, 0, T, right)
        expect_part(0, n, T)
        pass_on(1, n, me, 0, T, left)
        expect_part(1, n, T)
        pass_on(2, n, me, 0, T, sibling)
        expect_part(2, n, T)

    wait('og0-0')
    pass_on(3, 0, left, 0, T, sibling)
    expect_part(3, 0, T)
    wait('og1-0')
    pass_on(4, 0, right, 0, T, sibling)
    expect_part(4, 0, T)
    wait('og5-0')
    pass_on(7, 0, facing, 0, T, sibling)
    expect_part(7, 0, T)

    wait('stats')
    inverses = []
    for i in range(N):
        means = get(stats, 0, i)
        mean = jnp.sum(means, axis=0, keepdims=True) * (1.0 / N)
        apart = means - mean
        spread = jnp.sum(get(stats, 1, i), axis=0, keepdims=True) + T * jnp.sum(apart * apart, axis=0, keepdims=True)
        inverse = lax.rsqrt(spread * (1.0 / width) + norm_eps)
        inverses.append(inverse)
        normed_tile = (at[:, rows(i)] - mean) * inverse
        at[:, rows(i)] = normed_tile
        normed[rows(i), :] = jnp.transpose(normed_tile)

    wait('g')
    for i in range(N):
        gate = jnp.transpose(g[rows(i), :].astype(F32))
        gt[:, rows(i)] = gate
        gated[:, rows(i)] = (at[:, rows(i)] * gate).astype(BF16)

    def weight_part(n):
        terms = jnp.dot(gated[...], og[:, columns[n]], preferred_element_type=F32)
        for i in range(2):
            block = jnp.transpose(terms[:, i * T : (i + 1) * T]).astype(BF16)
            wg[4 * n + 2 * i : 4 * n + 2 * i + 2] = block.reshape(2, NY, 16, T)
        ry[y, parts[n]] = wg[parts[n], y]
        for d in range(1, NY):
            yy = lax.rem(y + d, NY)
            send(wg.at[parts[n], yy], ry.at[y, parts[n]], w_send.at[2 + n], w_recv.at[2 + n], y_peer(yy))
        part_of = ry.at[pl.ds(0, NY - 1), parts[n]]
        expect('ry%d' % n, part_of, w_recv.at[2 + n])
        expect('ry%d sent' % n, part_of, w_send.at[2 + n])

    for kind in (2, 3, 4, 7):
        wait('og%d-0' % kind)
    weight_part(0)
    wait('w z')
    for d in range(1, NY):
        send(w.at[:, y], w.at[:, y], w_send.at[1], w_recv.at[1], y_peer(lax.rem(y + d, NY)))
    expect('w y', w.at[:, pl.ds(0, NY - 1)], w_recv.at[1])
    expect('w y sent', w.at[:, pl.ds(0, NY - 1)], w_send.at[1])
    for n in range(1, 4):
        wait('og0-%d' % n)
        pass_on(5, n, left, 0, T // 2, right)
        expect_part(5, n, T // 2)
        wait('og1-%d' % n)
        pass_on(6, n, right, T // 2, T // 2, left)
        expect_part(6, n, T // 2)
        pass_on(3, n, left, 0, T, sibling)
        expect_part(3, n, T)
        pass_on(4, n, right, 0, T, sibling)
        expect_part(4, n, T)
    for n in range(1, 4):
        wait('og5-%d' % n)
        pass_on(7, n, facing, 0, T // 2, sibling)
        expect_part(7, n, T // 2)
        wait('og6-%d' % n)
        pass_on(8, n, facing, T // 2, T // 2, sibling)
        expect_part(8, n, T // 2)
        for kind in (2, 3, 4, 7, 8):
            wait('og%d-%d' % (kind, n))
        weight_part(n)

    wait('w y')
    weight = w[...].reshape(width, T)
    for i in range(N):
        gated_grad = jnp.dot(og[rows(i), :], weight, preferred_element_type=F32)
        dg[rows(i), :] = (gated_grad * normed[rows(i), :]).astype(BF16)
        normed_grad = jnp.transpose(gated_grad) * gt[:, rows(i)]
        ngt[:, rows(i)] = normed_grad
        put(grad_stats, 0, i, jnp.sum(normed_grad, axis=0, keepdims=True))
        put(grad_stats, 1, i, jnp.sum(normed_grad * at[:, rows(i)], axis=0, keepdims=True))
    share('grad stats', 6, grad_stats)

    for n, part in enumerate(parts):
        wait('ry%d' % n)
        total = ry[0, part].astype(F32)
        for m in range(1, NY):
            total = total + ry[m, part].astype(F32)
        zs[part] = total.astype(BF16)
        for d in range(4):
            zz = 4 * n + lax.rem(z + d, 4)

            @pl.when(zz != z)
            def _():
                send(zs.at[zz], rz.at[z], w_send.at[6], w_recv.at[6], z_peer(zz))

    rz[z] = zs[z]
    expect('rz', rz.at[pl.ds(0, NZ - 1)], w_recv.at[6])
    expect('rz sent', rz.at[pl.ds(0, NZ - 1)], w_send.at[6])
    deliver('dg', 0, dg, dg_out)

    wait('grad stats')
    for i in range(N):
        grad_mean = jnp.sum(get(grad_stats, 0, i), axis=0, keepdims=True) * (1.0 / width)
        cross = jnp.sum(get(grad_stats, 1, i), axis=0, keepdims=True) * (1.0 / width)
        dat[:, rows(i)] = (inverses[i] * (ngt[:, rows(i)] - grad_mean - at[:, rows(i)] * cross)).astype(BF16)

    for j in range(N):
        lo, hi = j * T, min(j + BAND + 1, N) * T
        dv[rows(j), :] = lax.dot_general(
            probs[rows(j), lo:hi], dat[:, lo:hi], NT, preferred_element_type=F32
        ).astype(BF16)
    deliver('dv', 1, dv, dv_out)
    for i in range(N):
        lo, hi = max(0, i - BAND) * T, (i + 1) * T
        for j in range(max(0, i - BAND), i + 1):
            prob_grad = jnp.dot(v[rows(j), :], dat[:, rows(i)], preferred_element_type=F32)
            ds[rows(j), rows(i)] = (prob_grad * slope[rows(j), rows(i)]).astype(BF16)
        dq[rows(i), :] = jnp.transpose(
            jnp.dot(kt[:, lo:hi], ds[lo:hi, rows(i)], preferred_element_type=F32)
        ).astype(BF16)
    deliver('dq', 2, dq, dq_out)

    for j in range(N):
        lo, hi = j * T, min(j + BAND + 1, N) * T
        dk[rows(j), :] = jnp.dot(ds[rows(j), lo:hi], q[lo:hi, :], preferred_element_type=F32).astype(BF16)
    deliver('dk', 3, dk, dk_out)

    for name in list(expected):
        if name[:2] not in ('dv', 'dq', 'dk', 'rz'):
            wait(name)
    wait('rz')
    total = rz[0].astype(F32)
    for n in range(1, NZ):
        total = total + rz[n].astype(F32)
    fin[...] = total * (1.0 / T)
    pltpu.make_async_copy(fin, wg_out.at[:, dyn(me)], own_sem).start()
    for d in range(1, N):
        send(fin, wg_out.at[:, dyn(me)], out_send.at[4], out_recv.at[4], seq_peer(lax.rem(me + d, N)))
    rest = wg_out.at[:, pl.ds(0, (N - 1) * T)]
    expect('fin', fin, own_sem)
    expect('dw', rest, out_recv.at[4])
    expect('dw sent', rest, out_send.at[4])

    for name in list(expected):
        wait(name)


def settle(*refs):
    sems = refs[10]
    copies = [pltpu.make_async_copy(refs[n], refs[5 + n], sems.at[n]) for n in range(5)]
    for copy in copies:
        copy.start()
    for copy in copies:
        copy.wait()


def shards(queries, keys, values, gates, out_grad, out_weight, time_bias, lengths, stamps):
    width = N * T
    event = pltpu.VMEM((T, width), BF16)
    block = pltpu.VMEM((width, T), BF16)
    across16 = pltpu.VMEM((T, width), BF16)
    across32 = pltpu.VMEM((T, width), F32)
    hbm = pl.BlockSpec(memory_space=pl.ANY)
    away = pl.BlockSpec(memory_space=pltpu.HBM)
    outs = pl.pallas_call(
        kernel,
        out_shape=(event, event, event, event, pltpu.VMEM((16, width), F32)),
        in_specs=[hbm] * 9,
        out_specs=(hbm,) * 5,
        scratch_shapes=[
            block, block, block, block,
            pltpu.VMEM((width, width), BF16),
            pltpu.VMEM((NZ, NY, 16, T), BF16),
            pltpu.VMEM((N, 1, T), jnp.int32),
            pltpu.VMEM((N, 8, 2 * T), F32), pltpu.VMEM((N, 8, 2 * T), F32),
            across16, across16,
            across32, across32, across32,
            across16, across16,
            pltpu.VMEM((width, T), F32),
            pltpu.VMEM((width, width), BF16),
            pltpu.VMEM((width, width), F32),
            pltpu.VMEM((width, width), BF16),
            block, block, block, block,
            pltpu.VMEM((NZ, NY, 16, T), BF16),
            pltpu.VMEM((NY, NZ, 16, T), BF16),
            pltpu.VMEM((NZ, 16, T), BF16),
            pltpu.VMEM((NZ, 16, T), BF16),
            pltpu.VMEM((16, T), F32),
            pltpu.VMEM((T, width), F32), pltpu.VMEM((16, width), F32), pltpu.VMEM((8, T), BF16),
            pltpu.SMEM((1, 4), jnp.int32), pltpu.VMEM((1, T), jnp.int32),
            pltpu.SemaphoreType.DMA((7,)),
            pltpu.SemaphoreType.DMA((7,)),
            pltpu.SemaphoreType.DMA((36,)),
            pltpu.SemaphoreType.DMA((36,)),
            pltpu.SemaphoreType.DMA((7,)),
            pltpu.SemaphoreType.DMA((7,)),
            pltpu.SemaphoreType.DMA((5,)),
            pltpu.SemaphoreType.DMA((5,)),
            pltpu.SemaphoreType.DMA,
            pltpu.SemaphoreType.DMA((5,)),
            pltpu.SemaphoreType.REGULAR,
        ],
        compiler_params=pltpu.CompilerParams(
            collective_id=0, has_side_effects=True, vmem_limit_bytes=48 * 1024 * 1024
        ),
    )(
        *(
            pltpu.with_memory_space_constraint(a, pltpu.HBM)
            for a in (queries, keys, values, gates, out_grad, out_weight, time_bias.T, lengths, stamps.reshape(1, T))
        )
    )
    return pl.pallas_call(
        settle,
        out_shape=[jax.ShapeDtypeStruct(o.shape, o.dtype) for o in outs],
        in_specs=[hbm] * 5,
        out_specs=[away] * 5,
        scratch_shapes=[pltpu.SemaphoreType.DMA((5,))],
        compiler_params=pltpu.CompilerParams(vmem_limit_bytes=4 * 1024 * 1024),
    )(*(pltpu.with_memory_space_constraint(o, pltpu.VMEM) for o in outs))


def solution(mesh):
    events = P(("dp", "seq"), None)
    return jax.shard_map(
        shards,
        mesh=mesh,
        in_specs=(
            events, events, events, events, events, P("dp", None), P(), P("dp", None), P(("dp", "seq")),
        ),
        out_specs=(events, events, events, events, P("dp", None)),
        check_vma=False,
    )
```

```python
import functools

import jax
import jax.numpy as jnp
from jax import lax
from jax.experimental import pallas as pl
from jax.experimental.pallas import tpu as pltpu
from jax.sharding import PartitionSpec as P

norm_eps = 1e-06
MESH = pl.DeviceIdType.MESH
F32 = jnp.float32
BF16 = jnp.bfloat16
T = 128
N = 8
NY = 4
NZ = 16
HUB = 11
BAND = 4
NT = (((1,), (1,)), ((), ()))


def rows(i):
    return pl.ds(i * T, T)


def dyn(i):
    return pl.ds(pl.multiple_of(i * T, T), T)


def kernel(
    q_in, k_in, v_in, g_in, og_hbm, w_hbm, tb_hbm, len_hbm, st_hbm,
    dq_out, dk_out, dv_out, dg_out, wg_out,
    q, k, v, g, og, w, stamps, stats, grad_stats,
    kt, vt, ngt, gt, at, dat, gated, normed, probs, slope, ds,
    dq, dk, dv, dg, wg, ry, zs, rz, fin,
    og_in, w_in, tb_in, len_in, st_in,
    in_send, in_recv, og_send, og_recv, w_send, w_recv, out_send, out_recv, own_sem, load_sem, ready,
):
    dp, me = lax.axis_index("dp"), lax.axis_index("seq")
    z, y = lax.div(dp, NY), lax.rem(dp, NY)
    chip, core = lax.div(me, 2), lax.rem(me, 2)
    left, right = lax.rem(me + N - 2, N), lax.rem(me + 2, N)
    facing = lax.rem(me + 4, N)
    sibling = 2 * chip + 1 - core
    width = N * T

    def seq_peer(s):
        return (dp, s)

    def z_peer(zz):
        return (zz * NY + y, me)

    def y_peer(yy):
        return (z * NY + yy, me)

    def send(src, dst, ssem, rsem, device):
        pltpu.make_async_remote_copy(
            src_ref=src, dst_ref=dst, send_sem=ssem, recv_sem=rsem, device_id=device, device_id_type=MESH
        ).start()

    def greet(first, last, sem, peer):
        def one(n, carry):
            pl.semaphore_signal(sem, inc=1, device_id=peer(n), device_id_type=MESH)
            return carry

        lax.fori_loop(first, last, one, 0)

    expected = {}

    def expect(name, ref, sem):
        expected[name] = (ref, sem)

    def wait(name):
        ref, sem = expected.pop(name)
        pltpu.make_async_copy(ref, ref, sem).wait()

    others = q.at[pl.ds(0, (N - 1) * T), :]

    def collect(n, src, dst):
        pltpu.make_async_copy(src.at[:, dyn(me)], dst.at[dyn(me), :], in_recv.at[n]).start()
        for d in range(1, N):
            peer = lax.rem(me + d, N)
            send(src.at[:, dyn(peer)], dst.at[dyn(me), :], in_send.at[n], in_recv.at[n], seq_peer(peer))

    def share(name, n, ref):
        for d in range(1, N):
            send(ref.at[me], ref.at[me], in_send.at[n], in_recv.at[n], seq_peer(lax.rem(me + d, N)))
        expect(name, ref.at[pl.ds(0, N - 1)], in_recv.at[n])
        expect(name + ' sent', ref.at[pl.ds(0, N - 1)], in_send.at[n])

    def deliver(name, n, src, dst):
        pltpu.make_async_copy(src.at[dyn(me), :], dst.at[:, dyn(me)], out_recv.at[n]).start()
        for d in range(1, N):
            peer = lax.rem(me + d, N)
            send(src.at[dyn(peer), :], dst.at[:, dyn(me)], out_send.at[n], out_recv.at[n], seq_peer(peer))
        expect(name, dst, out_recv.at[n])
        expect(name + ' sent', others, out_send.at[n])

    columns = [pl.ds(n * 2 * T, 2 * T) for n in range(4)]
    parts = [pl.ds(n * 4, 4) for n in range(4)]

    def pass_on(kind, n, owner, first, count, peer):
        ref = og.at[pl.ds(pl.multiple_of(owner * T + first, T // 2), count), columns[n]]
        send(ref, ref, og_send.at[4 * kind + n], og_recv.at[4 * kind + n], seq_peer(peer))

    def expect_part(kind, n, count):
        size = og.at[pl.ds(0, count), pl.ds(0, 2 * T)]
        expect('og%d-%d' % (kind, n), size, og_recv.at[4 * kind + n])
        expect('og%d-%d sent' % (kind, n), size, og_send.at[4 * kind + n])

    loads = [
        pltpu.make_async_copy(src, dst, load_sem.at[n])
        for n, (src, dst) in enumerate(
            ((og_hbm, og_in), (w_hbm, w_in), (tb_hbm, tb_in), (len_hbm, len_in), (st_hbm, st_in))
        )
    ]
    for load in loads:
        load.start()

    barrier = pltpu.get_barrier_semaphore()
    for d in range(1, N):
        pl.semaphore_signal(barrier, inc=1, device_id=seq_peer(lax.rem(me + d, N)), device_id_type=MESH)
    greet(y + 1, NY, barrier, y_peer)

    @pl.when(z != HUB)
    def _():
        pl.semaphore_signal(barrier, inc=1, device_id=z_peer(HUB), device_id_type=MESH)

    for load in loads:
        load.wait()
    og[dyn(me), :] = og_in[...].astype(BF16)
    stamps[me] = st_in[...]
    w[z, y] = w_in[:, dyn(me)].astype(BF16)

    pl.semaphore_wait(barrier, N - 1 + y + jnp.where(z == HUB, NZ - 1, 0))
    share('stamps', 0, stamps)
    collect(1, q_in, q)
    greet(0, y, ready, y_peer)

    @pl.when(z == HUB)
    def _():
        for d in range(1, NZ):
            pl.semaphore_signal(ready, inc=1, device_id=z_peer(lax.rem(z + d, NZ)), device_id_type=MESH)

    heads_of = tb_in[...].astype(F32)
    mine = jnp.where(lax.broadcasted_iota(jnp.int32, heads_of.shape, 0) == me, heads_of, 0.0)
    table = jnp.broadcast_to(jnp.sum(mine, axis=0, keepdims=True), (T, T))
    place = lax.broadcasted_iota(jnp.int32, (1, N * T), 1)
    end = jnp.int32(0)
    start = jnp.zeros((1, N * T), jnp.int32)
    for n in range(len_in.shape[1]):
        end = end + len_in[0, n]
        start = jnp.where(place >= end, end, start)
    below = lax.broadcasted_iota(jnp.int32, (T, T), 0)
    across = lax.broadcasted_iota(jnp.int32, (T, T), 1)
    def spread_weight():
        answers = NY - 1 - y + jnp.where(z == HUB, 0, 1)

        @pl.when(answers > 0)
        def _():
            pl.semaphore_wait(ready, answers)

        for d in range(1, NZ):
            send(w.at[z, y], w.at[z, y], w_send.at[0], w_recv.at[0], z_peer(lax.rem(z + d, NZ)))

    def start_ring():
        pass_on(0, 0, me, 0, T, right)
        pass_on(1, 0, me, 0, T, left)
        pass_on(5, 0, me, 0, T, facing)
        pass_on(2, 0, me, 0, T, sibling)

    @pl.when(z < NZ // 4)
    def _():
        collect(2, k_in, k)
        collect(3, v_in, v)
        collect(4, g_in, g)
        start_ring()

    @pl.when((z >= NZ // 4) & (z < NZ // 2))
    def _():
        collect(2, k_in, k)
        collect(3, v_in, v)
        spread_weight()
        collect(4, g_in, g)
        start_ring()

    @pl.when(z >= NZ // 2)
    def _():
        collect(2, k_in, k)
        spread_weight()
        collect(3, v_in, v)
        collect(4, g_in, g)
        start_ring()

    for n, (name, dst) in enumerate((('q', q), ('k', k), ('v', v), ('g', g))):
        expect(name, dst, in_recv.at[1 + n])
        expect(name + ' sent', others, in_send.at[1 + n])
    for kind in (0, 1, 5, 2):
        expect_part(kind, 0, T)
    expect('w z', w.at[pl.ds(0, NZ - 1), 0], w_recv.at[0])
    expect('w z sent', w.at[pl.ds(0, NZ - 1), 0], w_send.at[0])

    wait('stamps')
    wait('q')
    wait('k')
    for i in range(N):
        query_stamps = stamps[i, 0:1, :]
        for j in range(max(0, i - BAND), i + 1):
            key_stamps = jnp.transpose(jnp.broadcast_to(stamps[j, 0:1, :], (T, T)))
            bucket = jnp.clip(query_stamps - key_stamps, 0, T - 1)
            bias = jnp.take_along_axis(table, bucket, axis=1)
            score = lax.dot_general(k[rows(j), :], q[rows(i), :], NT, preferred_element_type=F32) + bias
            allowed = below >= start[:, i * T : (i + 1) * T] - j * T
            if i == j:
                allowed = allowed & (below <= across)
            sigma = jnp.where(allowed, 0.5 * jnp.tanh(0.5 * score) + 0.5, 0.0)
            prob = score * sigma
            probs[rows(j), rows(i)] = prob.astype(BF16)
            slope[rows(j), rows(i)] = sigma + prob * (1.0 - sigma)

    wait('v')
    for i in range(N):
        vt[:, rows(i)] = jnp.transpose(v[rows(i), :])
        kt[:, rows(i)] = jnp.transpose(k[rows(i), :])

    def put(ref, n, i, value):
        row, col = 4 * n + i // 2, (i % 2) * T
        ref[me, row : row + 1, col : col + T] = value

    def get(ref, n, i):
        row, col = 4 * n + i // 2, (i % 2) * T
        return ref[:, row, col : col + T]

    for i in range(N):
        lo, hi = max(0, i - BAND) * T, (i + 1) * T
        attended = jnp.dot(vt[:, lo:hi], probs[lo:hi, rows(i)], preferred_element_type=F32)
        at[:, rows(i)] = attended
        mean = jnp.sum(attended, axis=0, keepdims=True) * (1.0 / T)
        centred = attended - mean
        put(stats, 0, i, mean)
        put(stats, 1, i, jnp.sum(centred * centred, axis=0, keepdims=True))
    share('stats', 5, stats)
    pl.when(z < NZ // 4)(spread_weight)
    for n in range(1, 4):
        pass_on(0, n, me, 0, T, right)
        expect_part(0, n, T)
        pass_on(1, n, me, 0, T, left)
        expect_part(1, n, T)
        pass_on(2, n, me, 0, T, sibling)
        expect_part(2, n, T)

    wait('og0-0')
    pass_on(3, 0, left, 0, T, sibling)
    expect_part(3, 0, T)
    wait('og1-0')
    pass_on(4, 0, right, 0, T, sibling)
    expect_part(4, 0, T)
    wait('og5-0')
    pass_on(7, 0, facing, 0, T, sibling)
    expect_part(7, 0, T)

    wait('stats')
    inverses = []
    for i in range(N):
        means = get(stats, 0, i)
        mean = jnp.sum(means, axis=0, keepdims=True) * (1.0 / N)
        apart = means - mean
        spread = jnp.sum(get(stats, 1, i), axis=0, keepdims=True) + T * jnp.sum(apart * apart, axis=0, keepdims=True)
        inverse = lax.rsqrt(spread * (1.0 / width) + norm_eps)
        inverses.append(inverse)
        normed_tile = (at[:, rows(i)] - mean) * inverse
        at[:, rows(i)] = normed_tile
        normed[rows(i), :] = jnp.transpose(normed_tile)

    wait('g')
    for i in range(N):
        gate = jnp.transpose(g[rows(i), :].astype(F32))
        gt[:, rows(i)] = gate
        gated[:, rows(i)] = (at[:, rows(i)] * gate).astype(BF16)

    def weight_part(n):
        terms = jnp.dot(gated[...], og[:, columns[n]], preferred_element_type=F32)
        for i in range(2):
            block = jnp.transpose(terms[:, i * T : (i + 1) * T]).astype(BF16)
            wg[4 * n + 2 * i : 4 * n + 2 * i + 2] = block.reshape(2, NY, 16, T)
        ry[y, parts[n]] = wg[parts[n], y]
        for d in range(1, NY):
            yy = lax.rem(y + d, NY)
            send(wg.at[parts[n], yy], ry.at[y, parts[n]], w_send.at[2 + n], w_recv.at[2 + n], y_peer(yy))
        part_of = ry.at[pl.ds(0, NY - 1), parts[n]]
        expect('ry%d sent' % n, part_of, w_send.at[2 + n])

    for kind in (2, 3, 4, 7):
        wait('og%d-0' % kind)
    weight_part(0)
    wait('w z')
    for d in range(1, NY):
        send(w.at[:, y], w.at[:, y], w_send.at[1], w_recv.at[1], y_peer(lax.rem(y + d, NY)))
    expect('w y', w.at[:, pl.ds(0, NY - 1)], w_recv.at[1])
    expect('w y sent', w.at[:, pl.ds(0, NY - 1)], w_send.at[1])
    for n in range(1, 4):
        wait('og0-%d' % n)
        pass_on(5, n, left, 0, T // 2, right)
        expect_part(5, n, T // 2)
        wait('og1-%d' % n)
        pass_on(6, n, right, T // 2, T // 2, left)
        expect_part(6, n, T // 2)
        pass_on(3, n, left, 0, T, sibling)
        expect_part(3, n, T)
        pass_on(4, n, right, 0, T, sibling)
        expect_part(4, n, T)
    def sum_part(n):
        landed = ry.at[pl.ds(0, NY - 1), parts[n]]
        pltpu.make_async_copy(landed, landed, w_recv.at[2 + n]).wait()
        total = ry[0, parts[n]].astype(F32)
        for m in range(1, NY):
            total = total + ry[m, parts[n]].astype(F32)
        zs[parts[n]] = total.astype(BF16)
        for d in range(4):
            zz = 4 * n + lax.rem(z + d, 4)

            @pl.when(zz != z)
            def _():
                send(zs.at[zz], rz.at[z], w_send.at[6], w_recv.at[6], z_peer(zz))

    @pl.when(z >= NZ // 4)
    def _():
        sum_part(0)

    for n in range(1, 4):
        wait('og5-%d' % n)
        pass_on(7, n, facing, 0, T // 2, sibling)
        expect_part(7, n, T // 2)
        wait('og6-%d' % n)
        pass_on(8, n, facing, T // 2, T // 2, sibling)
        expect_part(8, n, T // 2)
        for kind in (2, 3, 4, 7, 8):
            wait('og%d-%d' % (kind, n))
        weight_part(n)

    wait('w y')
    weight = w[...].reshape(width, T)
    for i in range(N):
        gated_grad = jnp.dot(og[rows(i), :], weight, preferred_element_type=F32)
        dg[rows(i), :] = (gated_grad * normed[rows(i), :]).astype(BF16)
        normed_grad = jnp.transpose(gated_grad) * gt[:, rows(i)]
        ngt[:, rows(i)] = normed_grad
        put(grad_stats, 0, i, jnp.sum(normed_grad, axis=0, keepdims=True))
        put(grad_stats, 1, i, jnp.sum(normed_grad * at[:, rows(i)], axis=0, keepdims=True))
    share('grad stats', 6, grad_stats)

    @pl.when(z >= NZ // 4)
    def _():
        for n in range(1, 4):
            sum_part(n)

    deliver('dg', 0, dg, dg_out)

    @pl.when(z < NZ // 4)
    def _():
        for n in range(4):
            sum_part(n)

    rz[z] = zs[z]
    expect('rz', rz.at[pl.ds(0, NZ - 1)], w_recv.at[6])
    expect('rz sent', rz.at[pl.ds(0, NZ - 1)], w_send.at[6])

    wait('grad stats')
    for i in range(N):
        grad_mean = jnp.sum(get(grad_stats, 0, i), axis=0, keepdims=True) * (1.0 / width)
        cross = jnp.sum(get(grad_stats, 1, i), axis=0, keepdims=True) * (1.0 / width)
        dat[:, rows(i)] = (inverses[i] * (ngt[:, rows(i)] - grad_mean - at[:, rows(i)] * cross)).astype(BF16)

    for j in range(N):
        lo, hi = j * T, min(j + BAND + 1, N) * T
        dv[rows(j), :] = lax.dot_general(
            probs[rows(j), lo:hi], dat[:, lo:hi], NT, preferred_element_type=F32
        ).astype(BF16)

    deliver('dv', 1, dv, dv_out)
    for i in range(N):
        lo, hi = max(0, i - BAND) * T, (i + 1) * T
        for j in range(max(0, i - BAND), i + 1):
            prob_grad = jnp.dot(v[rows(j), :], dat[:, rows(i)], preferred_element_type=F32)
            ds[rows(j), rows(i)] = (prob_grad * slope[rows(j), rows(i)]).astype(BF16)
        dq[rows(i), :] = jnp.transpose(
            jnp.dot(kt[:, lo:hi], ds[lo:hi, rows(i)], preferred_element_type=F32)
        ).astype(BF16)
    deliver('dq', 2, dq, dq_out)

    for j in range(N):
        lo, hi = j * T, min(j + BAND + 1, N) * T
        dk[rows(j), :] = jnp.dot(ds[rows(j), lo:hi], q[lo:hi, :], preferred_element_type=F32).astype(BF16)
    deliver('dk', 3, dk, dk_out)

    for name in list(expected):
        if name[:2] not in ('dv', 'dq', 'dk', 'rz'):
            wait(name)
    wait('rz')
    total = rz[0].astype(F32)
    for n in range(1, NZ):
        total = total + rz[n].astype(F32)
    fin[...] = total * (1.0 / T)
    pltpu.make_async_copy(fin, wg_out.at[:, dyn(me)], own_sem).start()
    for d in range(1, N):
        send(fin, wg_out.at[:, dyn(me)], out_send.at[4], out_recv.at[4], seq_peer(lax.rem(me + d, N)))
    rest = wg_out.at[:, pl.ds(0, (N - 1) * T)]
    expect('fin', fin, own_sem)
    expect('dw', rest, out_recv.at[4])
    expect('dw sent', rest, out_send.at[4])

    for name in list(expected):
        wait(name)


def settle(*refs):
    sems = refs[10]
    copies = [pltpu.make_async_copy(refs[n], refs[5 + n], sems.at[n]) for n in range(5)]
    for copy in copies:
        copy.start()
    for copy in copies:
        copy.wait()


def shards(queries, keys, values, gates, out_grad, out_weight, time_bias, lengths, stamps):
    width = N * T
    event = pltpu.VMEM((T, width), BF16)
    block = pltpu.VMEM((width, T), BF16)
    across16 = pltpu.VMEM((T, width), BF16)
    across32 = pltpu.VMEM((T, width), F32)
    hbm = pl.BlockSpec(memory_space=pl.ANY)
    away = pl.BlockSpec(memory_space=pltpu.HBM)
    outs = pl.pallas_call(
        kernel,
        out_shape=(event, event, event, event, pltpu.VMEM((16, width), F32)),
        in_specs=[hbm] * 9,
        out_specs=(hbm,) * 5,
        scratch_shapes=[
            block, block, block, block,
            pltpu.VMEM((width, width), BF16),
            pltpu.VMEM((NZ, NY, 16, T), BF16),
            pltpu.VMEM((N, 1, T), jnp.int32),
            pltpu.VMEM((N, 8, 2 * T), F32), pltpu.VMEM((N, 8, 2 * T), F32),
            across16, across16,
            across32, across32, across32,
            across16, across16,
            pltpu.VMEM((width, T), F32),
            pltpu.VMEM((width, width), BF16),
            pltpu.VMEM((width, width), F32),
            pltpu.VMEM((width, width), BF16),
            block, block, block, block,
            pltpu.VMEM((NZ, NY, 16, T), BF16),
            pltpu.VMEM((NY, NZ, 16, T), BF16),
            pltpu.VMEM((NZ, 16, T), BF16),
            pltpu.VMEM((NZ, 16, T), BF16),
            pltpu.VMEM((16, T), F32),
            pltpu.VMEM((T, width), F32), pltpu.VMEM((16, width), F32), pltpu.VMEM((8, T), BF16),
            pltpu.SMEM((1, 4), jnp.int32), pltpu.VMEM((1, T), jnp.int32),
            pltpu.SemaphoreType.DMA((7,)),
            pltpu.SemaphoreType.DMA((7,)),
            pltpu.SemaphoreType.DMA((36,)),
            pltpu.SemaphoreType.DMA((36,)),
            pltpu.SemaphoreType.DMA((7,)),
            pltpu.SemaphoreType.DMA((7,)),
            pltpu.SemaphoreType.DMA((5,)),
            pltpu.SemaphoreType.DMA((5,)),
            pltpu.SemaphoreType.DMA,
            pltpu.SemaphoreType.DMA((5,)),
            pltpu.SemaphoreType.REGULAR,
        ],
        compiler_params=pltpu.CompilerParams(
            collective_id=0, has_side_effects=True, vmem_limit_bytes=48 * 1024 * 1024
        ),
    )(
        *(
            pltpu.with_memory_space_constraint(a, pltpu.HBM)
            for a in (queries, keys, values, gates, out_grad, out_weight, time_bias.T, lengths, stamps.reshape(1, T))
        )
    )
    return pl.pallas_call(
        settle,
        out_shape=[jax.ShapeDtypeStruct(o.shape, o.dtype) for o in outs],
        in_specs=[hbm] * 5,
        out_specs=[away] * 5,
        scratch_shapes=[pltpu.SemaphoreType.DMA((5,))],
        compiler_params=pltpu.CompilerParams(vmem_limit_bytes=4 * 1024 * 1024),
    )(*(pltpu.with_memory_space_constraint(o, pltpu.VMEM) for o in outs))


def solution(mesh):
    events = P(("dp", "seq"), None)
    return jax.shard_map(
        shards,
        mesh=mesh,
        in_specs=(
            events, events, events, events, events, P("dp", None), P(), P("dp", None), P(("dp", "seq")),
        ),
        out_specs=(events, events, events, events, P("dp", None)),
        check_vma=False,
    )
```
